256 devices in a mesh: row: 16 (over x, y_lo, core), col: 16 (over z, y_hi).
Axes of the slice: x: 4, y: 4 (y_hi: 2, y_lo: 2; y = y_hi * 2 + y_lo), z: 8, core: 2. Of those that a mesh axis runs over, the one named last changes fastest.
Arguments:
- embeddings: bfloat16 [49152, 128], P(('row', 'col')), as said below
- recordings: int32 [49152], P(('row', 'col')), may hold values from 0 to 6143
- start_basis: bfloat16 [32, 49152], P(None, ('row', 'col')), may hold values from -6 to 6
Outputs:
- basis: float32 [32, 49152], P(None, ('row', 'col'))
The draws below stay inside these ranges and needn't reach their ends.
Inputs may be any that keep to these rules, and one draw needn't show every extreme that they name: `embeddings`: one embedding per speaker segment.
All inputs are finite; a program needn't handle non-finite values.
Results may differ from the reference program's by a relative error of at most 0.0057.
Values may be sent and summed in bfloat16 or wider, within the bound.
A program may use at most 64 MiB of HBM per device.

```python
import math
import jax
import jax.numpy as jnp
from jax import lax

E = 128
K = 32
NPTS = 49152
NREC = 6144


def record_ids(key):
    return jax.random.randint(jax.random.fold_in(key, 11), (NPTS,), 0, NREC)


def speaker_values(key):
    owners = record_ids(key)
    inner = jax.random.fold_in(key, 5)
    first_key, second_key = jax.random.split(inner, 2)
    centres = jax.random.normal(first_key, (NREC, E), jnp.float32)
    noise = jax.random.normal(second_key, (NPTS, E), jnp.float32)
    return 0.65 * centres[owners] + noise


def draw_recordings(key, part):
    return record_ids(key).astype(jnp.int32)


def draw_embeddings(key, part):
    values = speaker_values(key)
    return values.astype(jnp.bfloat16)


def draw_start_basis(key, part):
    values = speaker_values(key)
    key = jax.random.fold_in(key, 37)
    mix_key, noise_key = jax.random.split(key, 2)
    mixing = jax.random.normal(mix_key, (E, K), jnp.float32)
    noise = jax.random.normal(noise_key, (K, NPTS), jnp.float32)
    projected = jnp.dot(values, mixing, precision=lax.Precision.HIGHEST) / jnp.sqrt(jnp.float32(E))
    result = jnp.clip(noise + 1.5 * projected.T, -6.0, 6.0)
    return result.astype(jnp.bfloat16)


def setup_inputs(seed: int = 0) -> dict:
    seeds = jax.random.split(jax.random.key(seed), 4)
    embeddings = draw_embeddings(jax.random.fold_in(seeds[3], 71), 0)
    recordings = draw_recordings(jax.random.fold_in(seeds[3], 71), 0)
    start_basis = draw_start_basis(jax.random.fold_in(seeds[3], 71), 0)
    return {"embeddings": embeddings, "recordings": recordings, "start_basis": start_basis}


def unit_rows(embeddings):
    values = embeddings.astype(jnp.float32)
    width = values.shape[1]
    scale = lax.rsqrt(lax.optimization_barrier(jnp.mean(values * values, axis=1, keepdims=True)) + 1e-06) / math.sqrt(width)
    return (values * scale).astype(jnp.bfloat16)

def affinity_of(cosine, same_rec, width):
    tau_value = 2.5 / math.sqrt(width)
    beta_value = 2.0 * math.sqrt(width)
    weights = jnp.maximum(jnp.exp(beta_value * (cosine - tau_value)) - 1.0, 0.0)
    return jnp.where(same_rec, jnp.zeros_like(weights), weights)

def reference(embeddings, recordings, start_basis):
    units = unit_rows(embeddings)
    block_len = math.gcd(NPTS, 512)
    block_count = NPTS // block_len

    def block_weights(index):
        start = (index * block_len).astype(jnp.int32)
        row_units = lax.dynamic_slice_in_dim(units, start, block_len, 0)
        row_ids = lax.dynamic_slice_in_dim(recordings, start, block_len, 0)
        cosine = jnp.dot(row_units.astype(jnp.float32), units.T.astype(jnp.float32), preferred_element_type=jnp.float32)
        return affinity_of(cosine, row_ids[:, None] == recordings[None, :], E)

    def degree_block(index):
        return 1.0 + lax.optimization_barrier(jnp.sum(block_weights(index), axis=1))
    indices = jnp.arange(block_count).astype(jnp.int32)
    degree = lax.map(degree_block, indices).reshape(NPTS)
    scaled = (start_basis.astype(jnp.float32) * lax.rsqrt(degree)[None, :]).astype(jnp.bfloat16)

    def image_block(index):
        weights = block_weights(index).astype(jnp.bfloat16)
        part = jnp.dot(scaled.astype(jnp.float32), weights.T.astype(jnp.float32), preferred_element_type=jnp.float32)
        start = (index * block_len).astype(jnp.int32)
        row_degree = lax.dynamic_slice_in_dim(degree, start, block_len, 0)
        return part * lax.rsqrt(row_degree)[None, :]
    parts = lax.map(image_block, indices)
    image_rows = jnp.moveaxis(parts, 0, 1).reshape(K, NPTS)
    gram = jnp.dot(image_rows, image_rows.T, precision=lax.Precision.HIGHEST)
    factor_low = jnp.linalg.cholesky(gram)
    solved = jax.scipy.linalg.solve_triangular(factor_low, image_rows, lower=True)
    return solved * math.sqrt(NPTS)
```

```python
import math

import jax
import jax.numpy as jnp
from jax import lax
from jax.experimental import pallas as pl
from jax.experimental.pallas import tpu as pltpu
from jax.sharding import PartitionSpec as P

MESH = pl.DeviceIdType.MESH
SEG, E, K = 192, 128, 32
NX, NY, NZ = 4, 4, 8
NPTS = SEG * NX * NY * NZ * 2
SIDE = SEG * 16
UROWS, XROWS, ZROWS = 192, 208, 272
BETA = 2.0 * math.sqrt(E)
SCALE = BETA * math.log2(math.e)
THETA = math.exp(5.0)
PAIR = 2 * SEG
HI = lax.Precision.HIGHEST


def pair_tail(first, second):
    return first + pltpu.roll(second, 64, 1)


def kernel(emb, rec, basis, out, zbuf, xbuf, uc, uo, idc, ido, tile, racc, dpart, dbuf,
           scaled, isend, irecv, gsend, grecv, hsend, hrecv, ssem, rsem):
    r = lax.axis_index("row")
    c = lax.axis_index("col")
    x, y, z, k = r // 4, (c % 2) * 2 + (r // 2) % 2, c // 2, r % 2

    def dev(px, py, pz, pk):
        return (px * 4 + (py % 2) * 2 + pk, pz * 2 + py // 2)

    def zdev(dz, dk):
        return dev(x, y, (z + dz) % NZ, (k + dk) % 2)

    def xydev(dx, dy):
        return dev((x + dx) % NX, (y + dy) % NY, z, k)

    zpeers = [(dz, dk) for dz in (4, 3, 5, 2, 6, 1, 7, 0) for dk in (0, 1) if (dz, dk) != (0, 0)]
    xypeers = [(dx, dy) for dx in (2, 1, 3, 0) for dy in (2, 1, 3, 0) if (dx, dy) != (0, 0)]

    barrier = pltpu.get_barrier_semaphore()
    for p in zpeers:
        pl.semaphore_signal(barrier, inc=1, device_id=zdev(*p), device_id_type=MESH)
    for p in xypeers:
        pl.semaphore_signal(barrier, inc=1, device_id=xydev(*p), device_id_type=MESH)

    values = emb[...].astype(jnp.float32)
    scale = lax.rsqrt(jnp.mean(values * values, axis=1, keepdims=True) + 1e-06) / math.sqrt(E)
    units = (values * scale).astype(jnp.bfloat16)
    ids = rec[...]
    parts = []
    for lanes in (slice(0, 128), slice(128, 192)):
        piece = ids[:, lanes]
        if piece.shape[1] < 128:
            piece = jnp.concatenate([piece, jnp.zeros_like(piece)], axis=1)
        parts += [(piece >> 8).astype(jnp.float32), (piece & 255).astype(jnp.float32)]
    idrows = jnp.concatenate(parts + [jnp.zeros((12, 128), jnp.float32)], axis=0)
    start = basis[...].astype(jnp.float32)
    tail = jnp.concatenate([start[:, 128:192], jnp.zeros((K, 64), jnp.float32)], axis=1)
    message = jnp.concatenate(
        [units, idrows.astype(jnp.bfloat16), start[:, 0:128].astype(jnp.bfloat16), tail.astype(jnp.bfloat16)], axis=0
    )
    own = zbuf.at[k]
    own[...] = message
    xbuf[0] = message[0:XROWS]
    pl.semaphore_wait(barrier, 30)

    sends = []

    def push(src, dst, group, slot, to):
        copy = pltpu.make_async_remote_copy(
            src_ref=src, dst_ref=dst, send_sem=ssem.at[group, slot], recv_sem=rsem.at[group, slot],
            device_id=to, device_id_type=MESH,
        )
        copy.start()
        sends.append(copy)
        return copy

    def zslot(dz, dk):
        return ((NZ - dz) % NZ) * 2 + dk

    def xyslot(dx, dy):
        return ((NX - dx) % NX) * 4 + (NY - dy) % NY

    near = [1, 7, 2, 6, 3, 5, 4]
    direct, handed = {}, {}
    for dz in near:
        d = (NZ - dz) % NZ
        direct[d] = push(own, zbuf.at[2 * d + k], 0, d, zdev(dz, 0))
    handed[0] = push(own, own, 1, 0, zdev(0, 1))
    gathered = []
    for p in sorted(xypeers, key=lambda p: min(p[0], 4 - p[0]) + min(p[1], 4 - p[1])):
        s = xyslot(*p)
        gathered.append(push(zbuf.at[k, 0:XROWS], xbuf.at[s], 2, s, xydev(*p)))
    for d in near:
        direct[d].wait_recv()
        handed[d] = push(zbuf.at[2 * d + k], zbuf.at[2 * d + k], 1, d, zdev(0, 1))
    for d in handed:
        handed[d].wait_recv()
    for copy in gathered:
        copy.wait_recv()

    def lane_ids(buf, s):
        rows = buf[s, UROWS:XROWS].astype(jnp.float32)
        return rows[0:1] * 256.0 + rows[1:2], rows[2:3] * 256.0 + rows[3:4]

    for m in range(8):
        a, b = 2 * m, 2 * m + 1
        for buf, dst in ((zbuf, uc), (xbuf, uo)):
            dst[PAIR * m:PAIR * m + 128] = buf[a, 0:128]
            dst[PAIR * m + 128:PAIR * m + 256] = buf[b, 0:128]
            dst[PAIR * m + 256:PAIR * m + 320] = buf[a, 128:192]
            dst[PAIR * m + 320:PAIR * m + 384] = buf[b, 128:192]
        main_a, tail_a = lane_ids(xbuf, a)
        main_b, tail_b = lane_ids(xbuf, b)
        for t, row in enumerate((main_a, main_b, pair_tail(tail_a, tail_b))):
            ido[0:1, PAIR * m + 128 * t:PAIR * m + 128 * (t + 1)] = row
        main_a, tail_a = lane_ids(zbuf, a)
        main_b, tail_b = lane_ids(zbuf, b)
        for t, row in enumerate((main_a, main_b, pair_tail(tail_a, tail_b))):
            idc[PAIR * m + 128 * t:PAIR * m + 128 * (t + 1), :] = jnp.broadcast_to(row, (128, 128)).T

    racc[...] = jnp.zeros_like(racc)

    def chunk(n, carry):
        start_lane = pl.multiple_of(n * PAIR, PAIR)
        cosine = lax.dot_general(
            uc[...], uo[pl.ds(start_lane, PAIR), :], (((1,), (1,)), ((), ())),
            preferred_element_type=jnp.float32,
        )
        total = racc[...]
        for t in range(3):
            lanes = pl.ds(pl.multiple_of(start_lane + 128 * t, 128), 128)
            weights = jnp.maximum(jnp.exp2(cosine[:, 128 * t:128 * (t + 1)] * SCALE) - THETA, 0.0)
            weights = jnp.where(idc[...] == ido[0:1, lanes], 0.0, weights)
            tile[:, lanes] = weights.astype(jnp.bfloat16)
            total = total + weights
        racc[...] = total
        return carry

    lax.fori_loop(0, 8, chunk, 0)

    for d in range(8):
        place = (z + d) % NZ
        for t in range(3):
            block = racc[PAIR * d + 128 * t:PAIR * d + 128 * (t + 1), :].T
            dpart[pl.ds(place * 3 + t, 1), :] = jnp.sum(block, axis=0, keepdims=True)
    copies = []
    for p in zpeers:
        s = zslot(*p)
        copies.append(push(dpart, dbuf.at[s], 3, s, zdev(*p)))
    degree = dpart[...]
    for copy, p in zip(copies, zpeers):
        copy.wait_recv()
        degree = degree + dbuf[zslot(*p)]
    dbuf[0] = lax.rsqrt(1.0 + degree * (1.0 / THETA))

    for d in range(8):
        place = (z + d) % NZ
        a, b = 2 * d, 2 * d + 1
        pieces = (
            zbuf[a, 208:240].astype(jnp.float32),
            zbuf[b, 208:240].astype(jnp.float32),
            pair_tail(zbuf[a, 240:272].astype(jnp.float32), zbuf[b, 240:272].astype(jnp.float32)),
        )
        for t, piece in enumerate(pieces):
            row = dbuf[0, pl.ds(place * 3 + t, 1), :]
            scaled[:, PAIR * d + 128 * t:PAIR * d + 128 * (t + 1)] = (piece * row).astype(jnp.bfloat16)

    low = lax.broadcasted_iota(jnp.int32, (16, 128), 1) < 64
    copies = []
    for m in (5, 7, 4, 6, 3, 2, 1, 0):
        image = jnp.dot(scaled[...], tile[:, PAIR * m:PAIR * (m + 1)], preferred_element_type=jnp.float32)
        tails = image[:, 256:384]
        turned = pltpu.roll(tails, 64, 1)
        tail_a = jnp.where(low, tails[0:16], turned[16:32])
        tail_b = jnp.where(low, turned[0:16], tails[16:32])
        for s, main, packed in ((2 * m, image[:, 0:128], tail_a), (2 * m + 1, image[:, 128:256], tail_b)):
            isend[s, 0:32] = main.astype(isend.dtype)
            isend[s, 32:48] = packed.astype(isend.dtype)
            if s:
                dx, dy = s // 4, s % 4
                t = xyslot(dx, dy)
                copies.append((t, push(isend.at[s], irecv.at[t], 4, t, xydev(dx, dy))))
            else:
                held = jnp.concatenate([main, packed], axis=0)
    for t, copy in copies:
        copy.wait_recv()
        held = held + irecv[t].astype(jnp.float32)
    low32 = lax.broadcasted_iota(jnp.int32, (K, 128), 1) < 64
    rest = held[32:48]
    rest = jnp.concatenate([rest, pltpu.roll(rest, 64, 1)], axis=0)
    dmain = dbuf[0, pl.ds(z * 3 + k, 1), :]
    dtail = dbuf[0, pl.ds(z * 3 + 2, 1), :]
    dtail = jnp.where(k == 0, dtail, pltpu.roll(dtail, 64, 1))
    img0 = held[0:32] * (dmain * (1.0 / THETA))
    img1 = jnp.where(low32, rest * (dtail * (1.0 / THETA)), 0.0)

    nt = (((1,), (1,)), ((), ()))
    gram = lax.dot_general(img0, img0, nt, precision=HI, preferred_element_type=jnp.float32)
    gram = gram + lax.dot_general(img1, img1, nt, precision=HI, preferred_element_type=jnp.float32)
    gram = jnp.concatenate([gram[8 * g:8 * g + 8] for g in range(4)], axis=1)
    gsend[...] = gram
    copies = []
    for p in xypeers:
        s = xyslot(*p)
        copies.append((s, push(gsend, grecv.at[s], 5, s, xydev(*p))))
    for s, copy in copies:
        copy.wait_recv()
        gram = gram + grecv[s]
    hsend[...] = gram
    copies = []
    for p in zpeers:
        s = zslot(*p)
        copies.append((s, push(hsend, hrecv.at[s], 6, s, zdev(*p))))
    hrecv[0] = gram
    for s, copy in copies:
        copy.wait_recv()
    for s, copy in copies:
        gram = gram + hrecv[s]
    gram = jnp.concatenate([gram] + [pltpu.roll(gram, 128 - 32 * g, 1) for g in range(1, 4)], axis=0)

    lane = lax.broadcasted_iota(jnp.int32, (K, 128), 1)
    sub = lax.broadcasted_iota(jnp.int32, (K, 128), 0)
    side = jnp.where(lane < 64, img1, pltpu.roll(jnp.where(lane < 32, gram, 0.0), 64, 1))
    for j in range(K - 1):
        pivot = side[j:j + 1, 64 + j:65 + j]
        factor = jnp.where(sub > j, side[:, 64 + j:65 + j] * (1.0 / pivot), 0.0)
        img0 = img0 - factor * img0[j:j + 1]
        side = side - factor * side[j:j + 1]
    diag = jnp.sum(jnp.where(lane == sub + 64, side, 0.0), axis=1, keepdims=True)
    final = lax.rsqrt(diag) * math.sqrt(NPTS)
    out[:, 0:128] = img0 * final
    out[:, 128:192] = (side * final)[:, 0:64]
    for copy in sends:
        copy.wait_send()


def on_device(embeddings, recordings, start_basis):
    f32, bf16 = jnp.float32, jnp.bfloat16
    return pl.pallas_call(
        kernel,
        out_shape=jax.ShapeDtypeStruct((K, SEG), f32),
        in_specs=[pl.BlockSpec(memory_space=pltpu.VMEM)] * 3,
        out_specs=pl.BlockSpec(memory_space=pltpu.VMEM),
        scratch_shapes=[
            pltpu.VMEM((16, ZROWS, 128), bf16),
            pltpu.VMEM((16, XROWS, 128), bf16),
            pltpu.VMEM((SIDE, 128), bf16),
            pltpu.VMEM((SIDE, 128), bf16),
            pltpu.VMEM((SIDE, 128), f32),
            pltpu.VMEM((8, SIDE), f32),
            pltpu.VMEM((SIDE, SIDE), bf16),
            pltpu.VMEM((SIDE, 128), f32),
            pltpu.VMEM((24, 128), f32),
            pltpu.VMEM((16, 24, 128), f32),
            pltpu.VMEM((K, SIDE), bf16),
            pltpu.VMEM((16, 48, 128), bf16),
            pltpu.VMEM((16, 48, 128), bf16),
            pltpu.VMEM((8, 128), f32),
            pltpu.VMEM((16, 8, 128), f32),
            pltpu.VMEM((8, 128), f32),
            pltpu.VMEM((16, 8, 128), f32),
            pltpu.SemaphoreType.DMA((7, 16)),
            pltpu.SemaphoreType.DMA((7, 16)),
        ],
        compiler_params=pltpu.CompilerParams(
            collective_id=0, has_side_effects=True, vmem_limit_bytes=56 * 2**20
        ),
    )(embeddings, recordings.reshape(1, SEG), start_basis)


def solution(mesh):
    in_specs = (P(("row", "col"), None), P(("row", "col")), P(None, ("row", "col")))
    out_specs = P(None, ("row", "col"))
    return jax.shard_map(
        on_device, mesh=mesh, in_specs=in_specs, out_specs=out_specs, check_vma=False
    )
```

```python
import math

import jax
import jax.numpy as jnp
from jax import lax
from jax.experimental import pallas as pl
from jax.experimental.pallas import tpu as pltpu
from jax.sharding import PartitionSpec as P

MESH = pl.DeviceIdType.MESH
SEG, E, K = 192, 128, 32
NX, NY, NZ = 4, 4, 8
NPTS = SEG * NX * NY * NZ * 2
SIDE = SEG * 16
UROWS, XROWS = 192, 208
ZORDER = (0, 7, 1, 6, 2, 5, 3, 4)
XORDER = (
    (0, 0), (3, 0), (1, 0), (0, 3), (0, 1), (2, 0), (3, 3), (3, 1),
    (1, 3), (1, 1), (0, 2), (3, 2), (1, 2), (2, 3), (2, 1), (2, 2),
)
BETA = 2.0 * math.sqrt(E)
SCALE = BETA * math.log2(math.e)
THETA = math.exp(5.0)
PAIR = 2 * SEG
HI = lax.Precision.HIGHEST


def pair_tail(first, second):
    return first + pltpu.roll(second, 64, 1)


def kernel(emb, rec, basis, out, zbuf, xbuf, bbuf, uc, uo, idc, ido, tile, racc, dpart, dbuf,
           scaled, isend, irecv, gsend, grecv, hsend, hrecv, ssem, rsem):
    r = lax.axis_index("row")
    c = lax.axis_index("col")
    x, y, z, k = r // 4, (c % 2) * 2 + (r // 2) % 2, c // 2, r % 2

    def dev(px, py, pz, pk):
        return (px * 4 + (py % 2) * 2 + pk, pz * 2 + py // 2)

    def zdev(dz, dk):
        return dev(x, y, (z + dz) % NZ, (k + dk) % 2)

    lead = k == 0

    def xydev(da, db):
        dx, dy = jnp.where(lead, da, db), jnp.where(lead, db, da)
        return dev((x + dx + NX) % NX, (y + dy + NY) % NY, z, k)

    zpeers = [(dz, dk) for dz in (4, 3, 5, 2, 6, 1, 7, 0) for dk in (0, 1) if (dz, dk) != (0, 0)]
    xypeers = [(dx, dy) for dx in (2, 1, 3, 0) for dy in (2, 1, 3, 0) if (dx, dy) != (0, 0)]

    barrier = pltpu.get_barrier_semaphore()
    for p in zpeers:
        pl.semaphore_signal(barrier, inc=1, device_id=zdev(*p), device_id_type=MESH)
    for p in xypeers:
        pl.semaphore_signal(barrier, inc=1, device_id=xydev(*p), device_id_type=MESH)

    values = emb[...].astype(jnp.float32)
    scale = lax.rsqrt(jnp.mean(values * values, axis=1, keepdims=True) + 1e-06) / math.sqrt(E)
    units = (values * scale).astype(jnp.bfloat16)
    ids = rec[...]
    parts = []
    for lanes in (slice(0, 128), slice(128, 192)):
        piece = ids[:, lanes]
        if piece.shape[1] < 128:
            piece = jnp.concatenate([piece, jnp.zeros_like(piece)], axis=1)
        parts += [(piece >> 8).astype(jnp.float32), (piece & 255).astype(jnp.float32)]
    idrows = jnp.concatenate(parts + [jnp.zeros((12, 128), jnp.float32)], axis=0)
    start = basis[...].astype(jnp.float32)
    tail = jnp.concatenate([start[:, 128:192], jnp.zeros((K, 64), jnp.float32)], axis=1)
    own = zbuf.at[k]
    own[...] = jnp.concatenate([units, idrows.astype(jnp.bfloat16)], axis=0)
    bown = bbuf.at[k]
    bown[...] = jnp.concatenate([start[:, 0:128], tail], axis=0).astype(jnp.bfloat16)

    racc[...] = jnp.zeros_like(racc)
    sends = []
    pl.semaphore_wait(barrier, 30)

    def push(src, dst, group, slot, to):
        copy = pltpu.make_async_remote_copy(
            src_ref=src, dst_ref=dst, send_sem=ssem.at[group, slot], recv_sem=rsem.at[group, slot],
            device_id=to, device_id_type=MESH,
        )
        copy.start()
        sends.append(copy)
        return copy

    def zslot(dz, dk):
        return ((NZ - dz) % NZ) * 2 + dk

    def xyslot(dx, dy):
        return ((NX - dx) % NX) * 4 + (NY - dy) % NY

    hop, relayed, plane = {}, {}, {}

    def zblock(d):
        return zbuf.at[2 * (d % NZ) + k]

    def zhop(d, step):
        t = (d - step) % NZ
        hop[t] = push(zblock(d), zblock(t), 0, t, zdev(step, 0))

    def relay(d):
        relayed[d] = push(zblock(d), zblock(d), 1, d, zdev(0, 1))

    def pblock(da, db):
        return own if (da, db) == (0, 0) else xbuf.at[da * 4 + db]

    def phop(da, db, sa, sb):
        t = ((da - sa) % 4, (db - sb) % 4)
        plane[t] = push(pblock(da, db), xbuf.at[t[0] * 4 + t[1]], 2, t[0] * 4 + t[1], xydev(sa, sb))

    zhop(0, 2)
    zhop(0, -2)
    phop(0, 0, 1, 0)
    phop(0, 0, -1, 0)
    zhop(0, 1)
    zhop(0, -1)
    relay(0)
    phop(0, 0, 0, 1)
    phop(0, 0, 0, -1)
    phop(0, 0, 2, 0)
    plane[3, 0].wait_recv()
    for step in (1, -1, 2):
        phop(3, 0, 0, step)
    plane[1, 0].wait_recv()
    for step in (1, -1, 2):
        phop(1, 0, 0, step)
    hop[6].wait_recv()
    zhop(6, 1)
    hop[2].wait_recv()
    zhop(2, -1)
    turn = jnp.where(lead, 6, 2)
    hop[4] = push(zblock(turn), zblock(4), 0, 4, zdev(jnp.where(lead, 2, NZ - 2), 0))
    relay(6)
    relay(2)
    hop[7].wait_recv()
    relay(7)
    hop[1].wait_recv()
    relay(1)
    plane[0, 1].wait_recv()
    phop(0, 1, 0, -1)
    plane[2, 0].wait_recv()
    for step in (1, -1, 2):
        phop(2, 0, 0, step)
    plane[0, 3].wait_recv()

    def lane_ids(buf, s):
        rows = buf[s, UROWS:XROWS].astype(jnp.float32)
        return rows[0:1] * 256.0 + rows[1:2], rows[2:3] * 256.0 + rows[3:4]

    def repack(buf, a, b, dst, m):
        dst[PAIR * m:PAIR * m + 128] = buf[a, 0:128]
        dst[PAIR * m + 128:PAIR * m + 256] = buf[b, 0:128]
        dst[PAIR * m + 256:PAIR * m + 320] = buf[a, 128:192]
        dst[PAIR * m + 320:PAIR * m + 384] = buf[b, 128:192]
        main_a, tail_a = lane_ids(buf, a)
        main_b, tail_b = lane_ids(buf, b)
        return [(PAIR * m + 128 * t, row) for t, row in enumerate((main_a, main_b, pair_tail(tail_a, tail_b)))]

    def take_z(m):
        d = ZORDER[m]
        relayed[d].wait_recv()
        for at, row in repack(zbuf, 2 * d, 2 * d + 1, uc, m):
            idc[at:at + 128, :] = jnp.broadcast_to(row, (128, 128)).T

    def take_xy(m):
        first, second = XORDER[2 * m], XORDER[2 * m + 1]
        for at, row in repack(xbuf, first[0] * 4 + first[1], second[0] * 4 + second[1], uo, m):
            ido[0:1, at:at + 128] = row

    def affinity(rows, n):
        lane0 = pl.multiple_of(2 * PAIR * n, 2 * PAIR)
        cosine = lax.dot_general(
            uc[rows, :], uo[pl.ds(lane0, 2 * PAIR), :], (((1,), (1,)), ((), ())),
            preferred_element_type=jnp.float32,
        )
        total = racc[rows, :]
        for t in range(6):
            lanes = pl.ds(pl.multiple_of(lane0 + 128 * t, 128), 128)
            weights = jnp.maximum(jnp.exp2(cosine[:, 128 * t:128 * (t + 1)] * SCALE) - THETA, 0.0)
            weights = jnp.where(idc[rows, :] == ido[0:1, lanes], 0.0, weights)
            tile[rows, lanes] = weights.astype(jnp.bfloat16)
            total = total + weights
        racc[rows, :] = total

    def two(rows, n):
        def body(i, carry):
            affinity(rows, n + i)
            return carry

        lax.fori_loop(0, 2, body, 0)

    near, far = slice(0, 5 * PAIR), slice(5 * PAIR, 8 * PAIR)
    xbuf[0] = own[...]
    for m in range(2):
        take_xy(m)
    for m in range(5):
        take_z(m)
    affinity(near, 0)
    for d in (5, 3, 4):
        hop[d].wait_recv()
        relay(d)
    bases = []
    for dz, dk in zpeers:
        s = zslot(dz, dk)
        bases.append(push(bown, bbuf.at[2 * (s // 2) + k], 7, s, zdev(dz, dk)))
    for s in ((3, 3), (3, 1)):
        plane[s].wait_recv()
    for m in (2, 3):
        take_xy(m)
    affinity(near, 1)
    for m in (5, 6, 7):
        take_z(m)
    two(far, 0)
    for s in ((1, 3), (1, 1), (0, 2), (3, 2)):
        plane[s].wait_recv()
    for m in (4, 5):
        take_xy(m)
    affinity(near, 2)
    for s in ((1, 2), (2, 3), (2, 1), (2, 2)):
        plane[s].wait_recv()
    for m in (6, 7):
        take_xy(m)
    affinity(near, 3)
    two(far, 2)

    for m, d in enumerate(ZORDER):
        place = (z + d) % NZ
        for t in range(3):
            block = racc[PAIR * m + 128 * t:PAIR * m + 128 * (t + 1), :].T
            dpart[pl.ds(place * 3 + t, 1), :] = jnp.sum(block, axis=0, keepdims=True)
    copies = []
    for p in zpeers:
        s = zslot(*p)
        copies.append(push(dpart, dbuf.at[s], 3, s, zdev(*p)))
    degree = dpart[...]
    for copy, p in zip(copies, zpeers):
        copy.wait_recv()
        degree = degree + dbuf[zslot(*p)]
    dbuf[0] = lax.rsqrt(1.0 + degree * (1.0 / THETA))

    for copy in bases:
        copy.wait_recv()
    for m, d in enumerate(ZORDER):
        place = (z + d) % NZ
        a, b = bbuf[2 * d].astype(jnp.float32), bbuf[2 * d + 1].astype(jnp.float32)
        pieces = (a[0:K], b[0:K], pair_tail(a[K:2 * K], b[K:2 * K]))
        for t, piece in enumerate(pieces):
            row = dbuf[0, pl.ds(place * 3 + t, 1), :]
            scaled[:, PAIR * m + 128 * t:PAIR * m + 128 * (t + 1)] = (piece * row).astype(jnp.bfloat16)

    low = lax.broadcasted_iota(jnp.int32, (16, 128), 1) < 64
    copies = []
    for m in range(7, -1, -1):
        image = jnp.dot(scaled[...], tile[:, PAIR * m:PAIR * (m + 1)], preferred_element_type=jnp.float32)
        tails = image[:, 256:384]
        turned = pltpu.roll(tails, 64, 1)
        tail_a = jnp.where(low, tails[0:16], turned[16:32])
        tail_b = jnp.where(low, turned[0:16], tails[16:32])
        for (da, db), main, packed in ((XORDER[2 * m], image[:, 0:128], tail_a), (XORDER[2 * m + 1], image[:, 128:256], tail_b)):
            s = da * 4 + db
            isend[s, 0:32] = main.astype(isend.dtype)
            isend[s, 32:48] = packed.astype(isend.dtype)
            if s:
                t = xyslot(da, db)
                copies.append((t, push(isend.at[s], irecv.at[t], 4, t, xydev(da, db))))
            else:
                held = jnp.concatenate([main, packed], axis=0)
    for t, copy in copies:
        copy.wait_recv()
        held = held + irecv[t].astype(jnp.float32)
    low32 = lax.broadcasted_iota(jnp.int32, (K, 128), 1) < 64
    rest = held[32:48]
    rest = jnp.concatenate([rest, pltpu.roll(rest, 64, 1)], axis=0)
    dmain = dbuf[0, pl.ds(z * 3 + k, 1), :]
    dtail = dbuf[0, pl.ds(z * 3 + 2, 1), :]
    dtail = jnp.where(k == 0, dtail, pltpu.roll(dtail, 64, 1))
    img0 = held[0:32] * (dmain * (1.0 / THETA))
    img1 = jnp.where(low32, rest * (dtail * (1.0 / THETA)), 0.0)

    nt = (((1,), (1,)), ((), ()))
    gram = lax.dot_general(img0, img0, nt, precision=HI, preferred_element_type=jnp.float32)
    gram = gram + lax.dot_general(img1, img1, nt, precision=HI, preferred_element_type=jnp.float32)
    gram = jnp.concatenate([gram[8 * g:8 * g + 8] for g in range(4)], axis=1)
    gsend[...] = gram
    copies = []
    for p in xypeers:
        s = xyslot(*p)
        copies.append((s, push(gsend, grecv.at[s], 5, s, xydev(*p))))
    for s, copy in copies:
        copy.wait_recv()
        gram = gram + grecv[s]
    hsend[...] = gram
    copies = []
    for p in zpeers:
        s = zslot(*p)
        copies.append((s, push(hsend, hrecv.at[s], 6, s, zdev(*p))))
    for s, copy in copies:
        copy.wait_recv()
    for s, copy in copies:
        gram = gram + hrecv[s]
    gram = jnp.concatenate([gram] + [pltpu.roll(gram, 128 - 32 * g, 1) for g in range(1, 4)], axis=0)

    lane = lax.broadcasted_iota(jnp.int32, (K, 128), 1)
    sub = lax.broadcasted_iota(jnp.int32, (K, 128), 0)
    side = jnp.where(lane < 64, img1, pltpu.roll(jnp.where(lane < 32, gram, 0.0), 64, 1))
    for j in range(K - 1):
        pivot = side[j:j + 1, 64 + j:65 + j]
        factor = jnp.where(sub > j, side[:, 64 + j:65 + j] * (1.0 / pivot), 0.0)
        img0 = img0 - factor * img0[j:j + 1]
        side = side - factor * side[j:j + 1]
    diag = jnp.sum(jnp.where(lane == sub + 64, side, 0.0), axis=1, keepdims=True)
    final = lax.rsqrt(diag) * math.sqrt(NPTS)
    out[:, 0:128] = img0 * final
    out[:, 128:192] = (side * final)[:, 0:64]
    for copy in sends:
        copy.wait_send()


def on_device(embeddings, recordings, start_basis):
    f32, bf16 = jnp.float32, jnp.bfloat16
    return pl.pallas_call(
        kernel,
        out_shape=jax.ShapeDtypeStruct((K, SEG), f32),
        in_specs=[pl.BlockSpec(memory_space=pltpu.VMEM)] * 3,
        out_specs=pl.BlockSpec(memory_space=pltpu.VMEM),
        scratch_shapes=[
            pltpu.VMEM((16, XROWS, 128), bf16),
            pltpu.VMEM((16, XROWS, 128), bf16),
            pltpu.VMEM((16, 2 * K, 128), bf16),
            pltpu.VMEM((SIDE, 128), bf16),
            pltpu.VMEM((SIDE, 128), bf16),
            pltpu.VMEM((SIDE, 128), f32),
            pltpu.VMEM((8, SIDE), f32),
            pltpu.VMEM((SIDE, SIDE), bf16),
            pltpu.VMEM((SIDE, 128), f32),
            pltpu.VMEM((24, 128), f32),
            pltpu.VMEM((16, 24, 128), f32),
            pltpu.VMEM((K, SIDE), bf16),
            pltpu.VMEM((16, 48, 128), bf16),
            pltpu.VMEM((16, 48, 128), bf16),
            pltpu.VMEM((8, 128), f32),
            pltpu.VMEM((16, 8, 128), f32),
            pltpu.VMEM((8, 128), f32),
            pltpu.VMEM((16, 8, 128), f32),
            pltpu.SemaphoreType.DMA((8, 16)),
            pltpu.SemaphoreType.DMA((8, 16)),
        ],
        compiler_params=pltpu.CompilerParams(
            collective_id=0, has_side_effects=True, vmem_limit_bytes=60 * 2**20
        ),
    )(embeddings, recordings.reshape(1, SEG), start_basis)


def solution(mesh):
    in_specs = (P(("row", "col"), None), P(("row", "col")), P(None, ("row", "col")))
    out_specs = P(None, ("row", "col"))
    return jax.shard_map(
        on_device, mesh=mesh, in_specs=in_specs, out_specs=out_specs, check_vma=False
    )
```

```python
import math

import jax
import jax.numpy as jnp
from jax import lax
from jax.experimental import pallas as pl
from jax.experimental.pallas import tpu as pltpu
from jax.sharding import PartitionSpec as P

MESH = pl.DeviceIdType.MESH
SEG, E, K = 192, 128, 32
NX, NY, NZ = 4, 4, 8
NPTS = SEG * NX * NY * NZ * 2
SIDE = SEG * 16
UROWS, XROWS = 192, 208
ZORDER = (0, 7, 1, 6, 2, 5, 3, 4)
XORDER = (
    (0, 0), (3, 0), (1, 0), (0, 3), (0, 1), (2, 0), (3, 3), (3, 1),
    (1, 3), (1, 1), (0, 2), (3, 2), (1, 2), (2, 3), (2, 1), (2, 2),
)
BETA = 2.0 * math.sqrt(E)
SCALE = BETA * math.log2(math.e)
THETA = math.exp(5.0)
PAIR = 2 * SEG
HI = lax.Precision.HIGHEST


def pair_tail(first, second):
    return first + pltpu.roll(second, 64, 1)


def kernel(emb, rec, basis, out, zbuf, xbuf, bbuf, uc, uo, idc, ido, tile, racc, dpart, dbuf,
           scaled, isend, irecv, gsend, grecv, hsend, hrecv, ssem, rsem):
    r = lax.axis_index("row")
    c = lax.axis_index("col")
    x, y, z, k = r // 4, (c % 2) * 2 + (r // 2) % 2, c // 2, r % 2

    def dev(px, py, pz, pk):
        return (px * 4 + (py % 2) * 2 + pk, pz * 2 + py // 2)

    def zdev(dz, dk):
        return dev(x, y, (z + dz) % NZ, (k + dk) % 2)

    lead = k == 0

    def xydev(da, db):
        dx, dy = jnp.where(lead, da, db), jnp.where(lead, db, da)
        return dev((x + dx + NX) % NX, (y + dy + NY) % NY, z, k)

    zpeers = [(dz, dk) for dz in (4, 3, 5, 2, 6, 1, 7, 0) for dk in (0, 1) if (dz, dk) != (0, 0)]
    xypeers = [(dx, dy) for dx in (2, 1, 3, 0) for dy in (2, 1, 3, 0) if (dx, dy) != (0, 0)]

    barrier = pltpu.get_barrier_semaphore()
    for p in ((2, 0), (6, 0), (1, 0), (7, 0), (0, 1)):
        pl.semaphore_signal(barrier, inc=1, device_id=zdev(*p), device_id_type=MESH)
    for p in ((2, 0), (0, 2), (1, 0), (3, 0), (0, 1), (0, 3)):
        pl.semaphore_signal(barrier, inc=1, device_id=xydev(*p), device_id_type=MESH)

    values = emb[...].astype(jnp.float32)
    scale = lax.rsqrt(jnp.mean(values * values, axis=1, keepdims=True) + 1e-06) / math.sqrt(E)
    units = (values * scale).astype(jnp.bfloat16)
    ids = rec[...]
    parts = []
    for lanes in (slice(0, 128), slice(128, 192)):
        piece = ids[:, lanes]
        if piece.shape[1] < 128:
            piece = jnp.concatenate([piece, jnp.zeros_like(piece)], axis=1)
        parts += [(piece >> 8).astype(jnp.float32), (piece & 255).astype(jnp.float32)]
    idrows = jnp.concatenate(parts + [jnp.zeros((12, 128), jnp.float32)], axis=0)
    start = basis[...].astype(jnp.float32)
    tail = jnp.concatenate([start[:, 128:192], jnp.zeros((K, 64), jnp.float32)], axis=1)
    own = zbuf.at[k]
    own[...] = jnp.concatenate([units, idrows.astype(jnp.bfloat16)], axis=0)
    bown = bbuf.at[k]
    bown[...] = jnp.concatenate([start[:, 0:128], tail], axis=0).astype(jnp.bfloat16)

    racc[...] = jnp.zeros_like(racc)
    sends = []
    pl.semaphore_wait(barrier, 11)

    def push(src, dst, group, slot, to):
        copy = pltpu.make_async_remote_copy(
            src_ref=src, dst_ref=dst, send_sem=ssem.at[group, slot], recv_sem=rsem.at[group, slot],
            device_id=to, device_id_type=MESH,
        )
        copy.start()
        sends.append(copy)
        return copy

    def zslot(dz, dk):
        return ((NZ - dz) % NZ) * 2 + dk

    def xyslot(dx, dy):
        return ((NX - dx) % NX) * 4 + (NY - dy) % NY

    hop, relayed, plane = {}, {}, {}

    def zblock(d):
        return zbuf.at[2 * (d % NZ) + k]

    def zhop(d, step):
        t = (d - step) % NZ
        hop[t] = push(zblock(d), zblock(t), 0, t, zdev(step, 0))

    def relay(d):
        relayed[d] = push(zblock(d), zblock(d), 1, d, zdev(0, 1))

    def pblock(da, db):
        return own if (da, db) == (0, 0) else xbuf.at[da * 4 + db]

    def phop(da, db, sa, sb):
        t = ((da - sa) % 4, (db - sb) % 4)
        plane[t] = push(pblock(da, db), xbuf.at[t[0] * 4 + t[1]], 2, t[0] * 4 + t[1], xydev(sa, sb))

    zhop(0, 2)
    zhop(0, -2)
    phop(0, 0, 1, 0)
    phop(0, 0, -1, 0)
    zhop(0, 1)
    zhop(0, -1)
    relay(0)
    phop(0, 0, 0, 1)
    phop(0, 0, 0, -1)
    phop(0, 0, 2, 0)
    plane[3, 0].wait_recv()
    for step in (1, -1, 2):
        phop(3, 0, 0, step)
    plane[1, 0].wait_recv()
    for step in (1, -1, 2):
        phop(1, 0, 0, step)
    hop[6].wait_recv()
    zhop(6, 1)
    hop[2].wait_recv()
    zhop(2, -1)
    turn = jnp.where(lead, 6, 2)
    hop[4] = push(zblock(turn), zblock(4), 0, 4, zdev(jnp.where(lead, 2, NZ - 2), 0))
    relay(6)
    relay(2)
    hop[7].wait_recv()
    relay(7)
    hop[1].wait_recv()
    relay(1)
    plane[0, 1].wait_recv()
    phop(0, 1, 0, -1)
    plane[2, 0].wait_recv()
    for step in (1, -1, 2):
        phop(2, 0, 0, step)
    seen = {(0, 0), (3, 0), (1, 0), (0, 1), (2, 0)}

    def lane_ids(buf, s):
        rows = buf[s, UROWS:XROWS].astype(jnp.float32)
        return rows[0:1] * 256.0 + rows[1:2], rows[2:3] * 256.0 + rows[3:4]

    def repack(buf, a, b, dst, m):
        dst[PAIR * m:PAIR * m + 128] = buf[a, 0:128]
        dst[PAIR * m + 128:PAIR * m + 256] = buf[b, 0:128]
        dst[PAIR * m + 256:PAIR * m + 320] = buf[a, 128:192]
        dst[PAIR * m + 320:PAIR * m + 384] = buf[b, 128:192]
        main_a, tail_a = lane_ids(buf, a)
        main_b, tail_b = lane_ids(buf, b)
        return [(PAIR * m + 128 * t, row) for t, row in enumerate((main_a, main_b, pair_tail(tail_a, tail_b)))]

    def take_z(m):
        d = ZORDER[m]
        relayed[d].wait_recv()
        for at, row in repack(zbuf, 2 * d, 2 * d + 1, uc, m):
            idc[at:at + 128, :] = jnp.broadcast_to(row, (128, 128)).T

    def take_xy(m):
        first, second = XORDER[2 * m], XORDER[2 * m + 1]
        for at, row in repack(xbuf, first[0] * 4 + first[1], second[0] * 4 + second[1], uo, m):
            ido[0:1, at:at + 128] = row

    def affinity(rows, n):
        lane0 = pl.multiple_of(2 * PAIR * n, 2 * PAIR)
        cosine = lax.dot_general(
            uc[rows, :], uo[pl.ds(lane0, 2 * PAIR), :], (((1,), (1,)), ((), ())),
            preferred_element_type=jnp.float32,
        )
        total = racc[rows, :]
        for t in range(6):
            lanes = pl.ds(pl.multiple_of(lane0 + 128 * t, 128), 128)
            weights = jnp.maximum(jnp.exp2(cosine[:, 128 * t:128 * (t + 1)] * SCALE) - THETA, 0.0)
            weights = jnp.where(idc[rows, :] == ido[0:1, lanes], 0.0, weights)
            tile[rows, lanes] = weights.astype(jnp.bfloat16)
            total = total + weights
        racc[rows, :] = total

    first, second = slice(0, 3 * PAIR), slice(3 * PAIR, 5 * PAIR)
    near, far = slice(0, 5 * PAIR), slice(5 * PAIR, 8 * PAIR)

    def take_plane(n):
        for s in XORDER[4 * n:4 * n + 4]:
            if s not in seen:
                plane[s].wait_recv()
        take_xy(2 * n)
        take_xy(2 * n + 1)

    xbuf[0] = own[...]
    take_plane(0)
    for m in range(3):
        take_z(m)
    affinity(first, 0)
    for m in (3, 4):
        take_z(m)
    affinity(second, 0)
    take_plane(1)
    affinity(near, 1)
    take_plane(2)
    affinity(near, 2)
    for d in (5, 3, 4):
        hop[d].wait_recv()
        relay(d)
    take_plane(3)
    affinity(near, 3)
    for m in (5, 6, 7):
        take_z(m)
    bases = []
    for dz, dk in zpeers:
        s = zslot(dz, dk)
        bases.append(push(bown, bbuf.at[2 * (s // 2) + k], 7, s, zdev(dz, dk)))

    def body(n, carry):
        affinity(far, n)
        return carry

    lax.fori_loop(0, 4, body, 0)

    for m, d in enumerate(ZORDER):
        place = (z + d) % NZ
        for t in range(3):
            block = racc[PAIR * m + 128 * t:PAIR * m + 128 * (t + 1), :].T
            dpart[pl.ds(place * 3 + t, 1), :] = jnp.sum(block, axis=0, keepdims=True)
    copies = []
    for p in zpeers:
        s = zslot(*p)
        copies.append(push(dpart, dbuf.at[s], 3, s, zdev(*p)))
    degree = dpart[...]
    for copy, p in zip(copies, zpeers):
        copy.wait_recv()
        degree = degree + dbuf[zslot(*p)]
    dbuf[0] = lax.rsqrt(1.0 + degree * (1.0 / THETA))

    for copy in bases:
        copy.wait_recv()
    for m, d in enumerate(ZORDER):
        place = (z + d) % NZ
        a, b = bbuf[2 * d].astype(jnp.float32), bbuf[2 * d + 1].astype(jnp.float32)
        pieces = (a[0:K], b[0:K], pair_tail(a[K:2 * K], b[K:2 * K]))
        for t, piece in enumerate(pieces):
            row = dbuf[0, pl.ds(place * 3 + t, 1), :]
            scaled[:, PAIR * m + 128 * t:PAIR * m + 128 * (t + 1)] = (piece * row).astype(jnp.bfloat16)

    low = lax.broadcasted_iota(jnp.int32, (16, 128), 1) < 64
    copies = []
    for m in range(7, -1, -1):
        image = jnp.dot(scaled[...], tile[:, PAIR * m:PAIR * (m + 1)], preferred_element_type=jnp.float32)
        tails = image[:, 256:384]
        turned = pltpu.roll(tails, 64, 1)
        tail_a = jnp.where(low, tails[0:16], turned[16:32])
        tail_b = jnp.where(low, turned[0:16], tails[16:32])
        for (da, db), main, packed in ((XORDER[2 * m], image[:, 0:128], tail_a), (XORDER[2 * m + 1], image[:, 128:256], tail_b)):
            s = da * 4 + db
            isend[s, 0:32] = main.astype(isend.dtype)
            isend[s, 32:48] = packed.astype(isend.dtype)
            if s:
                t = xyslot(da, db)
                copies.append((t, push(isend.at[s], irecv.at[t], 4, t, xydev(da, db))))
            else:
                held = jnp.concatenate([main, packed], axis=0)
    for t, copy in copies:
        copy.wait_recv()
        held = held + irecv[t].astype(jnp.float32)
    low32 = lax.broadcasted_iota(jnp.int32, (K, 128), 1) < 64
    rest = held[32:48]
    rest = jnp.concatenate([rest, pltpu.roll(rest, 64, 1)], axis=0)
    dmain = dbuf[0, pl.ds(z * 3 + k, 1), :]
    dtail = dbuf[0, pl.ds(z * 3 + 2, 1), :]
    dtail = jnp.where(k == 0, dtail, pltpu.roll(dtail, 64, 1))
    img0 = held[0:32] * (dmain * (1.0 / THETA))
    img1 = jnp.where(low32, rest * (dtail * (1.0 / THETA)), 0.0)

    nt = (((1,), (1,)), ((), ()))
    gram = lax.dot_general(img0, img0, nt, precision=HI, preferred_element_type=jnp.float32)
    gram = gram + lax.dot_general(img1, img1, nt, precision=HI, preferred_element_type=jnp.float32)
    gram = jnp.concatenate([gram[8 * g:8 * g + 8] for g in range(4)], axis=1)
    gsend[...] = gram
    copies = []
    for p in xypeers:
        s = xyslot(*p)
        copies.append((s, push(gsend, grecv.at[s], 5, s, xydev(*p))))
    for s, copy in copies:
        copy.wait_recv()
        gram = gram + grecv[s]
    hsend[...] = gram
    copies = []
    for p in zpeers:
        s = zslot(*p)
        copies.append((s, push(hsend, hrecv.at[s], 6, s, zdev(*p))))
    for s, copy in copies:
        copy.wait_recv()
    for s, copy in copies:
        gram = gram + hrecv[s]
    gram = jnp.concatenate([gram] + [pltpu.roll(gram, 128 - 32 * g, 1) for g in range(1, 4)], axis=0)

    lane = lax.broadcasted_iota(jnp.int32, (K, 128), 1)
    sub = lax.broadcasted_iota(jnp.int32, (K, 128), 0)
    side = jnp.where(lane < 64, img1, pltpu.roll(jnp.where(lane < 32, gram, 0.0), 64, 1))
    for j in range(K - 1):
        pivot = side[j:j + 1, 64 + j:65 + j]
        factor = jnp.where(sub > j, side[:, 64 + j:65 + j] * (1.0 / pivot), 0.0)
        img0 = img0 - factor * img0[j:j + 1]
        side = side - factor * side[j:j + 1]
    diag = jnp.sum(jnp.where(lane == sub + 64, side, 0.0), axis=1, keepdims=True)
    final = lax.rsqrt(diag) * math.sqrt(NPTS)
    out[:, 0:128] = img0 * final
    out[:, 128:192] = (side * final)[:, 0:64]
    for copy in sends:
        copy.wait_send()


def on_device(embeddings, recordings, start_basis):
    f32, bf16 = jnp.float32, jnp.bfloat16
    return pl.pallas_call(
        kernel,
        out_shape=jax.ShapeDtypeStruct((K, SEG), f32),
        in_specs=[pl.BlockSpec(memory_space=pltpu.VMEM)] * 3,
        out_specs=pl.BlockSpec(memory_space=pltpu.VMEM),
        scratch_shapes=[
            pltpu.VMEM((16, XROWS, 128), bf16),
            pltpu.VMEM((16, XROWS, 128), bf16),
            pltpu.VMEM((16, 2 * K, 128), bf16),
            pltpu.VMEM((SIDE, 128), bf16),
            pltpu.VMEM((SIDE, 128), bf16),
            pltpu.VMEM((SIDE, 128), f32),
            pltpu.VMEM((8, SIDE), f32),
            pltpu.VMEM((SIDE, SIDE), bf16),
            pltpu.VMEM((SIDE, 128), f32),
            pltpu.VMEM((24, 128), f32),
            pltpu.VMEM((16, 24, 128), f32),
            pltpu.VMEM((K, SIDE), bf16),
            pltpu.VMEM((16, 48, 128), bf16),
            pltpu.VMEM((16, 48, 128), bf16),
            pltpu.VMEM((8, 128), f32),
            pltpu.VMEM((16, 8, 128), f32),
            pltpu.VMEM((8, 128), f32),
            pltpu.VMEM((16, 8, 128), f32),
            pltpu.SemaphoreType.DMA((8, 16)),
            pltpu.SemaphoreType.DMA((8, 16)),
        ],
        compiler_params=pltpu.CompilerParams(
            collective_id=0, has_side_effects=True, vmem_limit_bytes=60 * 2**20
        ),
    )(embeddings, recordings.reshape(1, SEG), start_basis)


def solution(mesh):
    in_specs = (P(("row", "col"), None), P(("row", "col")), P(None, ("row", "col")))
    out_specs = P(None, ("row", "col"))
    return jax.shard_map(
        on_device, mesh=mesh, in_specs=in_specs, out_specs=out_specs, check_vma=False
    )
```

```python
import math

import jax
import jax.numpy as jnp
from jax import lax
from jax.experimental import pallas as pl
from jax.experimental.pallas import tpu as pltpu
from jax.sharding import PartitionSpec as P

MESH = pl.DeviceIdType.MESH
SEG, E, K = 192, 128, 32
NX, NY, NZ = 4, 4, 8
NPTS = SEG * NX * NY * NZ * 2
SIDE = SEG * 16
UROWS, XROWS = 192, 208
ZORDER = (0, 7, 1, 6, 2, 5, 3, 4)
XORDER = (
    (0, 0), (3, 0), (1, 0), (0, 3), (0, 1), (2, 0), (3, 3), (3, 1),
    (1, 3), (1, 1), (0, 2), (3, 2), (1, 2), (2, 3), (2, 1), (2, 2),
)
BETA = 2.0 * math.sqrt(E)
SCALE = BETA * math.log2(math.e)
THETA = math.exp(5.0)
PAIR = 2 * SEG
HI = lax.Precision.HIGHEST


def pair_tail(first, second):
    return first + pltpu.roll(second, 64, 1)


def kernel(emb_hbm, rec_hbm, basis_hbm, out, emb, rec, basis, zbuf, xbuf, bbuf, uc, uo, idc, ido, tile, racc, dnear, dfar, nbuf, fbuf, dinv,
           scaled, isend, irecv, gsend, grecv, hsend, hrecv, ssem, rsem, isem):
    r = lax.axis_index("row")
    c = lax.axis_index("col")
    x, y, z, k = r // 4, (c % 2) * 2 + (r // 2) % 2, c // 2, r % 2

    def dev(px, py, pz, pk):
        return (px * 4 + (py % 2) * 2 + pk, pz * 2 + py // 2)

    def zdev(dz, dk):
        return dev(x, y, (z + dz) % NZ, (k + dk) % 2)

    lead = k == 0

    def xydev(da, db):
        dx, dy = jnp.where(lead, da, db), jnp.where(lead, db, da)
        return dev((x + dx + NX) % NX, (y + dy + NY) % NY, z, k)

    zpeers = [(dz, dk) for dz in (4, 3, 5, 2, 6, 1, 7, 0) for dk in (0, 1) if (dz, dk) != (0, 0)]
    xypeers = [(dx, dy) for dx in (2, 1, 3, 0) for dy in (2, 1, 3, 0) if (dx, dy) != (0, 0)]

    barrier = pltpu.get_barrier_semaphore()
    for p in ((2, 0), (6, 0), (1, 0), (7, 0), (0, 1)):
        pl.semaphore_signal(barrier, inc=1, device_id=zdev(*p), device_id_type=MESH)
    for p in ((2, 0), (0, 2), (1, 0), (3, 0), (0, 1), (0, 3)):
        pl.semaphore_signal(barrier, inc=1, device_id=xydev(*p), device_id_type=MESH)

    loads = [
        pltpu.make_async_copy(src, dst, isem.at[i])
        for i, (src, dst) in enumerate(((emb_hbm, emb), (rec_hbm, rec), (basis_hbm, basis)))
    ]
    for load in loads:
        load.start()
    racc[...] = jnp.zeros_like(racc)
    for load in loads:
        load.wait()

    values = emb[...].astype(jnp.float32)
    scale = lax.rsqrt(jnp.mean(values * values, axis=1, keepdims=True) + 1e-06) / math.sqrt(E)
    units = (values * scale).astype(jnp.bfloat16)
    ids = rec[...]
    parts = []
    for lanes in (slice(0, 128), slice(128, 192)):
        piece = ids[:, lanes]
        if piece.shape[1] < 128:
            piece = jnp.concatenate([piece, jnp.zeros_like(piece)], axis=1)
        parts += [(piece >> 8).astype(jnp.float32), (piece & 255).astype(jnp.float32)]
    idrows = jnp.concatenate(parts + [jnp.zeros((12, 128), jnp.float32)], axis=0)
    start = basis[...].astype(jnp.float32)
    tail = jnp.concatenate([start[:, 128:192], jnp.zeros((K, 64), jnp.float32)], axis=1)
    own = zbuf.at[k]
    own[...] = jnp.concatenate([units, idrows.astype(jnp.bfloat16)], axis=0)
    bown = bbuf.at[k]
    bown[...] = jnp.concatenate([start[:, 0:128], tail], axis=0).astype(jnp.bfloat16)

    sends = []
    pl.semaphore_wait(barrier, 11)

    def push(src, dst, group, slot, to):
        copy = pltpu.make_async_remote_copy(
            src_ref=src, dst_ref=dst, send_sem=ssem.at[group, slot], recv_sem=rsem.at[group, slot],
            device_id=to, device_id_type=MESH,
        )
        copy.start()
        sends.append(copy)
        return copy

    def zslot(dz, dk):
        return ((NZ - dz) % NZ) * 2 + dk

    def xyslot(dx, dy):
        return ((NX - dx) % NX) * 4 + (NY - dy) % NY

    hop, relayed, plane = {}, {}, {}

    def zblock(d):
        return zbuf.at[2 * (d % NZ) + k]

    def zhop(d, step):
        t = (d - step) % NZ
        hop[t] = push(zblock(d), zblock(t), 0, t, zdev(step, 0))

    def relay(d):
        relayed[d] = push(zblock(d), zblock(d), 1, d, zdev(0, 1))

    def pblock(da, db):
        return own if (da, db) == (0, 0) else xbuf.at[da * 4 + db]

    def phop(da, db, sa, sb):
        t = ((da - sa) % 4, (db - sb) % 4)
        plane[t] = push(pblock(da, db), xbuf.at[t[0] * 4 + t[1]], 2, t[0] * 4 + t[1], xydev(sa, sb))

    zhop(0, 2)
    zhop(0, -2)
    phop(0, 0, 1, 0)
    phop(0, 0, -1, 0)
    zhop(0, 1)
    zhop(0, -1)
    relay(0)
    phop(0, 0, 0, 1)
    phop(0, 0, 0, -1)
    phop(0, 0, 2, 0)
    plane[3, 0].wait_recv()
    for step in (1, -1, 2):
        phop(3, 0, 0, step)
    plane[1, 0].wait_recv()
    for step in (1, -1, 2):
        phop(1, 0, 0, step)
    hop[6].wait_recv()
    zhop(6, 1)
    hop[2].wait_recv()
    zhop(2, -1)
    turn = jnp.where(lead, 6, 2)
    hop[4] = push(zblock(turn), zblock(4), 0, 4, zdev(jnp.where(lead, 2, NZ - 2), 0))
    relay(6)
    relay(2)
    hop[7].wait_recv()
    relay(7)
    hop[1].wait_recv()
    relay(1)
    plane[0, 1].wait_recv()
    phop(0, 1, 0, -1)
    plane[2, 0].wait_recv()
    for step in (1, -1, 2):
        phop(2, 0, 0, step)
    bases, handed = {}, {}

    def basis_to(dz):
        d = (NZ - dz) % NZ
        bases[d] = push(bown, bbuf.at[2 * d + k], 7, d, zdev(dz, 0))

    def basis_relay(d):
        if d:
            bases[d].wait_recv()
        handed[d] = push(bbuf.at[2 * d + k], bbuf.at[2 * d + k], 7, 8 + d, zdev(0, 1))

    for dz in (6, 2, 7, 1):
        basis_to(dz)
    seen = {(0, 0), (3, 0), (1, 0), (0, 1), (2, 0)}

    def lane_ids(buf, s):
        rows = buf[s, UROWS:XROWS].astype(jnp.float32)
        return rows[0:1] * 256.0 + rows[1:2], rows[2:3] * 256.0 + rows[3:4]

    def repack(buf, a, b, dst, m):
        dst[PAIR * m:PAIR * m + 128] = buf[a, 0:128]
        dst[PAIR * m + 128:PAIR * m + 256] = buf[b, 0:128]
        dst[PAIR * m + 256:PAIR * m + 320] = buf[a, 128:192]
        dst[PAIR * m + 320:PAIR * m + 384] = buf[b, 128:192]
        main_a, tail_a = lane_ids(buf, a)
        main_b, tail_b = lane_ids(buf, b)
        return [(PAIR * m + 128 * t, row) for t, row in enumerate((main_a, main_b, pair_tail(tail_a, tail_b)))]

    def take_z(m):
        d = ZORDER[m]
        relayed[d].wait_recv()
        for at, row in repack(zbuf, 2 * d, 2 * d + 1, uc, m):
            idc[at:at + 128, :] = jnp.broadcast_to(row, (128, 128)).T

    def take_xy(m):
        first, second = XORDER[2 * m], XORDER[2 * m + 1]
        for at, row in repack(xbuf, first[0] * 4 + first[1], second[0] * 4 + second[1], uo, m):
            ido[0:1, at:at + 128] = row

    def affinity(rows, n):
        lane0 = pl.multiple_of(2 * PAIR * n, 2 * PAIR)
        cosine = lax.dot_general(
            uc[rows, :], uo[pl.ds(lane0, 2 * PAIR), :], (((1,), (1,)), ((), ())),
            preferred_element_type=jnp.float32,
        )
        for at in range(rows.start, rows.stop, 16):
            part = slice(at, at + 16)
            total = racc[part, :]
            for t in range(6):
                lanes = pl.ds(pl.multiple_of(lane0 + 128 * t, 128), 128)
                piece = cosine[at - rows.start:at - rows.start + 16, 128 * t:128 * (t + 1)]
                weights = jnp.maximum(jnp.exp2(piece * SCALE) - THETA, 0.0)
                weights = jnp.where(idc[part, :] == ido[0:1, lanes], 0.0, weights)
                tile[part, lanes] = weights.astype(jnp.bfloat16)
                total = total + weights
            racc[part, :] = total

    first, second = slice(0, 3 * PAIR), slice(3 * PAIR, 5 * PAIR)
    near, far = slice(0, 5 * PAIR), slice(5 * PAIR, 8 * PAIR)

    def take_plane(n):
        for s in XORDER[4 * n:4 * n + 4]:
            if s not in seen:
                plane[s].wait_recv()
        take_xy(2 * n)
        take_xy(2 * n + 1)

    xbuf[0] = own[...]
    take_plane(0)
    for m in range(3):
        take_z(m)
    affinity(first, 0)
    for m in (3, 4):
        take_z(m)
    affinity(second, 0)
    take_plane(1)
    affinity(near, 1)
    take_plane(2)
    affinity(near, 2)
    for d in (5, 3, 4):
        hop[d].wait_recv()
        relay(d)
    for dz in (4, 3, 5):
        basis_to(dz)
    for d in (0, 7, 1, 6, 2):
        basis_relay(d)
    take_plane(3)
    affinity(near, 3)
    for m in (5, 6, 7):
        take_z(m)

    def row_sums(ms):
        sums = {}
        for m in ms:
            for t in range(3):
                block = racc[PAIR * m + 128 * t:PAIR * m + 128 * (t + 1), :].T
                sums[3 * ((ZORDER[m] + 2) % NZ) + t] = jnp.sum(block, axis=0, keepdims=True)
        return sums

    for row, value in row_sums(range(5)).items():
        dnear[row:row + 1, :] = value
    dnear[15:16, :] = jnp.zeros((1, 128), jnp.float32)
    near_copies = {p: push(dnear, nbuf.at[zslot(*p)], 3, zslot(*p), zdev(*p)) for p in zpeers}

    def body(n, carry):
        affinity(far, n)
        return carry

    lax.fori_loop(0, 4, body, 0)

    sums = row_sums(range(5, 8))
    rest = jnp.concatenate([sums[row] for row in range(15, 24)] + [jnp.zeros((7, 128), jnp.float32)], axis=0)
    dfar[...] = rest.astype(jnp.bfloat16)
    far_copies = {p: push(dfar, fbuf.at[zslot(*p)], 8, zslot(*p), zdev(*p)) for p in zpeers}
    for d in (5, 3, 4):
        basis_relay(d)
    degree = jnp.concatenate([dnear[0:15], rest[0:9]], axis=0)
    for dz in (0, 1, 7, 2, 6, 3, 5, 4):
        part = None
        for dk in ((1,) if dz == 0 else (0, 1)):
            near_copies[dz, dk].wait_recv()
            far_copies[dz, dk].wait_recv()
            slot = zslot(dz, dk)
            got = jnp.concatenate([nbuf[slot, 0:15], fbuf[slot].astype(jnp.float32)[0:9]], axis=0)
            part = got if part is None else part + got
        turn = 3 * dz
        if turn:
            part = jnp.concatenate([part[turn:24], part[0:turn]], axis=0)
        degree = degree + part
    dinv[...] = lax.rsqrt(1.0 + degree * (1.0 / THETA))

    for d in handed:
        handed[d].wait_recv()
    for m, d in enumerate(ZORDER):
        place = 3 * ((d + 2) % NZ)
        a, b = bbuf[2 * d].astype(jnp.float32), bbuf[2 * d + 1].astype(jnp.float32)
        pieces = (a[0:K], b[0:K], pair_tail(a[K:2 * K], b[K:2 * K]))
        for t, piece in enumerate(pieces):
            row = dinv[place + t:place + t + 1, :]
            scaled[:, PAIR * m + 128 * t:PAIR * m + 128 * (t + 1)] = (piece * row).astype(jnp.bfloat16)

    low = lax.broadcasted_iota(jnp.int32, (16, 128), 1) < 64
    copies = []
    for m in range(7, -1, -1):
        image = jnp.dot(scaled[...], tile[:, PAIR * m:PAIR * (m + 1)], preferred_element_type=jnp.float32)
        tails = image[:, 256:384]
        turned = pltpu.roll(tails, 64, 1)
        tail_a = jnp.where(low, tails[0:16], turned[16:32])
        tail_b = jnp.where(low, turned[0:16], tails[16:32])
        for (da, db), main, packed in ((XORDER[2 * m], image[:, 0:128], tail_a), (XORDER[2 * m + 1], image[:, 128:256], tail_b)):
            s = da * 4 + db
            isend[s, 0:32] = main.astype(isend.dtype)
            isend[s, 32:48] = packed.astype(isend.dtype)
            if s:
                t = xyslot(da, db)
                copies.append((t, push(isend.at[s], irecv.at[t], 4, t, xydev(da, db))))
            else:
                held = jnp.concatenate([main, packed], axis=0)
    for t, copy in copies:
        copy.wait_recv()
        held = held + irecv[t].astype(jnp.float32)
    low32 = lax.broadcasted_iota(jnp.int32, (K, 128), 1) < 64
    rest = held[32:48]
    rest = jnp.concatenate([rest, pltpu.roll(rest, 64, 1)], axis=0)
    dmain = dinv[pl.ds(6 + k, 1), :]
    dtail = dinv[8:9, :]
    dtail = jnp.where(k == 0, dtail, pltpu.roll(dtail, 64, 1))
    img0 = held[0:32] * (dmain * (1.0 / THETA))
    img1 = jnp.where(low32, rest * (dtail * (1.0 / THETA)), 0.0)

    nt = (((1,), (1,)), ((), ()))
    gram = lax.dot_general(img0, img0, nt, precision=HI, preferred_element_type=jnp.float32)
    gram = gram + lax.dot_general(img1, img1, nt, precision=HI, preferred_element_type=jnp.float32)
    gram = jnp.concatenate([gram[8 * g:8 * g + 8] for g in range(4)], axis=1)
    gsend[...] = gram
    copies = []
    for p in xypeers:
        s = xyslot(*p)
        copies.append((s, push(gsend, grecv.at[s], 5, s, xydev(*p))))
    for s, copy in copies:
        copy.wait_recv()
        gram = gram + grecv[s]
    hsend[...] = gram
    copies = []
    for p in zpeers:
        s = zslot(*p)
        copies.append((s, push(hsend, hrecv.at[s], 6, s, zdev(*p))))
    for s, copy in copies:
        copy.wait_recv()
    for s, copy in copies:
        gram = gram + hrecv[s]
    gram = jnp.concatenate([gram] + [pltpu.roll(gram, 128 - 32 * g, 1) for g in range(1, 4)], axis=0)

    lane = lax.broadcasted_iota(jnp.int32, (K, 128), 1)
    sub = lax.broadcasted_iota(jnp.int32, (K, 128), 0)
    side = jnp.where(lane < 64, img1, pltpu.roll(jnp.where(lane < 32, gram, 0.0), 64, 1))
    for j in range(0, K, 2):
        col_a = jnp.broadcast_to(side[:, 64 + j:65 + j], (K, 128))
        col_b = jnp.broadcast_to(side[:, 65 + j:66 + j], (K, 128))
        aa, ab, bb = col_a[j:j + 1], col_b[j:j + 1], col_b[j + 1:j + 2]
        ra = 1.0 / aa
        ratio = ab * ra
        rest = 1.0 / (bb - ab * ratio)
        fac_b = jnp.where(sub > j + 1, (col_b - col_a * ratio) * rest, 0.0)
        fac_a = jnp.where(sub > j, col_a * ra - fac_b * ratio, 0.0)
        img0 = img0 - (fac_a * img0[j:j + 1] + fac_b * img0[j + 1:j + 2])
        side = side - (fac_a * side[j:j + 1] + fac_b * side[j + 1:j + 2])
    diag = jnp.sum(jnp.where(lane == sub + 64, side, 0.0), axis=1, keepdims=True)
    final = lax.rsqrt(diag) * math.sqrt(NPTS)
    out[:, 0:128] = img0 * final
    out[:, 128:192] = (side * final)[:, 0:64]
    for copy in sends:
        copy.wait_send()


def on_device(embeddings, recordings, start_basis):
    f32, bf16 = jnp.float32, jnp.bfloat16
    return pl.pallas_call(
        kernel,
        out_shape=jax.ShapeDtypeStruct((K, SEG), f32),
        in_specs=[pl.BlockSpec(memory_space=pl.ANY)] * 3,
        out_specs=pl.BlockSpec(memory_space=pltpu.VMEM),
        scratch_shapes=[
            pltpu.VMEM((SEG, E), bf16),
            pltpu.VMEM((1, SEG), jnp.int32),
            pltpu.VMEM((K, SEG), bf16),
            pltpu.VMEM((16, XROWS, 128), bf16),
            pltpu.VMEM((16, XROWS, 128), bf16),
            pltpu.VMEM((16, 2 * K, 128), bf16),
            pltpu.VMEM((SIDE, 128), bf16),
            pltpu.VMEM((SIDE, 128), bf16),
            pltpu.VMEM((SIDE, 128), f32),
            pltpu.VMEM((8, SIDE), f32),
            pltpu.VMEM((SIDE, SIDE), bf16),
            pltpu.VMEM((SIDE, 128), f32),
            pltpu.VMEM((16, 128), f32),
            pltpu.VMEM((16, 128), bf16),
            pltpu.VMEM((16, 16, 128), f32),
            pltpu.VMEM((16, 16, 128), bf16),
            pltpu.VMEM((24, 128), f32),
            pltpu.VMEM((K, SIDE), bf16),
            pltpu.VMEM((16, 48, 128), bf16),
            pltpu.VMEM((16, 48, 128), bf16),
            pltpu.VMEM((8, 128), f32),
            pltpu.VMEM((16, 8, 128), f32),
            pltpu.VMEM((8, 128), f32),
            pltpu.VMEM((16, 8, 128), f32),
            pltpu.SemaphoreType.DMA((9, 16)),
            pltpu.SemaphoreType.DMA((9, 16)),
            pltpu.SemaphoreType.DMA((3,)),
        ],
        compiler_params=pltpu.CompilerParams(
            collective_id=0, has_side_effects=True, vmem_limit_bytes=60 * 2**20
        ),
    )(embeddings, recordings.reshape(1, SEG), start_basis)


def solution(mesh):
    in_specs = (P(("row", "col"), None), P(("row", "col")), P(None, ("row", "col")))
    out_specs = P(None, ("row", "col"))
    return jax.shard_map(
        on_device, mesh=mesh, in_specs=in_specs, out_specs=out_specs, check_vma=False
    )
```

```python
import math

import jax
import jax.numpy as jnp
from jax import lax
from jax.experimental import pallas as pl
from jax.experimental.pallas import tpu as pltpu
from jax.sharding import PartitionSpec as P

MESH = pl.DeviceIdType.MESH
SEG, E, K = 192, 128, 32
NX, NY, NZ = 4, 4, 8
NPTS = SEG * NX * NY * NZ * 2
SIDE = SEG * 16
UROWS, XROWS = 192, 208
ZORDER = (0, 7, 1, 6, 2, 5, 3, 4)
XORDER = (
    (0, 0), (3, 0), (1, 0), (0, 3), (0, 1), (2, 0), (3, 3), (3, 1),
    (1, 3), (1, 1), (0, 2), (3, 2), (1, 2), (2, 3), (2, 1), (2, 2),
)
BETA = 2.0 * math.sqrt(E)
SCALE = BETA * math.log2(math.e)
THETA = math.exp(5.0)
PAIR = 2 * SEG
HI = lax.Precision.HIGHEST


def pair_tail(first, second):
    return first + pltpu.roll(second, 64, 1)


def kernel(emb_hbm, rec_hbm, basis_hbm, out, emb, rec, basis, zbuf, xbuf, bbuf, uc, uo, idc, ido, tile, racc, dnear, dfar, nbuf, fbuf, dinv,
           scaled, isend, irecv, gsend, grecv, hsend, hrecv, ssem, rsem, isem):
    r = lax.axis_index("row")
    c = lax.axis_index("col")
    x, y, z, k = r // 4, (c % 2) * 2 + (r // 2) % 2, c // 2, r % 2

    def dev(px, py, pz, pk):
        return (px * 4 + (py % 2) * 2 + pk, pz * 2 + py // 2)

    def zdev(dz, dk):
        return dev(x, y, (z + dz) % NZ, (k + dk) % 2)

    lead = k == 0

    def xydev(da, db):
        dx, dy = jnp.where(lead, da, db), jnp.where(lead, db, da)
        return dev((x + dx + NX) % NX, (y + dy + NY) % NY, z, k)

    zpeers = [(dz, dk) for dz in (4, 3, 5, 2, 6, 1, 7, 0) for dk in (0, 1) if (dz, dk) != (0, 0)]
    xypeers = [(dx, dy) for dx in (2, 1, 3, 0) for dy in (2, 1, 3, 0) if (dx, dy) != (0, 0)]

    barrier = pltpu.get_barrier_semaphore()
    for p in ((2, 0), (6, 0), (1, 0), (7, 0), (0, 1)):
        pl.semaphore_signal(barrier, inc=1, device_id=zdev(*p), device_id_type=MESH)
    for p in ((2, 0), (0, 2), (1, 0), (3, 0), (0, 1), (0, 3)):
        pl.semaphore_signal(barrier, inc=1, device_id=xydev(*p), device_id_type=MESH)

    loads = [
        pltpu.make_async_copy(src, dst, isem.at[i])
        for i, (src, dst) in enumerate(((emb_hbm, emb), (rec_hbm, rec), (basis_hbm, basis)))
    ]
    for load in loads:
        load.start()
    racc[...] = jnp.zeros_like(racc)
    for load in loads:
        load.wait()

    values = emb[...].astype(jnp.float32)
    scale = lax.rsqrt(jnp.mean(values * values, axis=1, keepdims=True) + 1e-06) / math.sqrt(E)
    units = (values * scale).astype(jnp.bfloat16)
    ids = rec[...]
    parts = []
    for lanes in (slice(0, 128), slice(128, 192)):
        piece = ids[:, lanes]
        if piece.shape[1] < 128:
            piece = jnp.concatenate([piece, jnp.zeros_like(piece)], axis=1)
        parts += [(piece >> 8).astype(jnp.float32), (piece & 255).astype(jnp.float32)]
    idrows = jnp.concatenate(parts + [jnp.zeros((12, 128), jnp.float32)], axis=0)
    start = basis[...].astype(jnp.float32)
    tail = jnp.concatenate([start[:, 128:192], jnp.zeros((K, 64), jnp.float32)], axis=1)
    own = zbuf.at[k]
    own[...] = jnp.concatenate([units, idrows.astype(jnp.bfloat16)], axis=0)
    bown = bbuf.at[k]
    bown[...] = jnp.concatenate([start[:, 0:128], tail], axis=0).astype(jnp.bfloat16)

    sends = []
    pl.semaphore_wait(barrier, 11)

    def push(src, dst, group, slot, to):
        copy = pltpu.make_async_remote_copy(
            src_ref=src, dst_ref=dst, send_sem=ssem.at[group, slot], recv_sem=rsem.at[group, slot],
            device_id=to, device_id_type=MESH,
        )
        copy.start()
        sends.append(copy)
        return copy

    def zslot(dz, dk):
        return ((NZ - dz) % NZ) * 2 + dk

    def xyslot(dx, dy):
        return ((NX - dx) % NX) * 4 + (NY - dy) % NY

    hop, relayed, plane = {}, {}, {}

    def zblock(d):
        return zbuf.at[2 * (d % NZ) + k]

    def zhop(d, step):
        t = (d - step) % NZ
        hop[t] = push(zblock(d), zblock(t), 0, t, zdev(step, 0))

    def relay(d):
        relayed[d] = push(zblock(d), zblock(d), 1, d, zdev(0, 1))

    def pblock(da, db):
        return own if (da, db) == (0, 0) else xbuf.at[da * 4 + db]

    def phop(da, db, sa, sb):
        t = ((da - sa) % 4, (db - sb) % 4)
        plane[t] = push(pblock(da, db), xbuf.at[t[0] * 4 + t[1]], 2, t[0] * 4 + t[1], xydev(sa, sb))

    zhop(0, 2)
    zhop(0, -2)
    phop(0, 0, 1, 0)
    phop(0, 0, -1, 0)
    zhop(0, 1)
    zhop(0, -1)
    relay(0)
    phop(0, 0, 0, 1)
    phop(0, 0, 0, -1)
    phop(0, 0, 2, 0)
    plane[3, 0].wait_recv()
    for step in (1, -1, 2):
        phop(3, 0, 0, step)
    plane[1, 0].wait_recv()
    for step in (1, -1, 2):
        phop(1, 0, 0, step)
    def lane_ids(buf, s):
        rows = buf[s, UROWS:XROWS].astype(jnp.float32)
        return rows[0:1] * 256.0 + rows[1:2], rows[2:3] * 256.0 + rows[3:4]

    def repack(buf, a, b, dst, m):
        dst[PAIR * m:PAIR * m + 128] = buf[a, 0:128]
        dst[PAIR * m + 128:PAIR * m + 256] = buf[b, 0:128]
        dst[PAIR * m + 256:PAIR * m + 320] = buf[a, 128:192]
        dst[PAIR * m + 320:PAIR * m + 384] = buf[b, 128:192]
        main_a, tail_a = lane_ids(buf, a)
        main_b, tail_b = lane_ids(buf, b)
        return [(PAIR * m + 128 * t, row) for t, row in enumerate((main_a, main_b, pair_tail(tail_a, tail_b)))]

    def take_z(m):
        d = ZORDER[m]
        relayed[d].wait_recv()
        for at, row in repack(zbuf, 2 * d, 2 * d + 1, uc, m):
            idc[at:at + 128, :] = jnp.broadcast_to(row, (128, 128)).T

    def take_xy(m):
        first, second = XORDER[2 * m], XORDER[2 * m + 1]
        for at, row in repack(xbuf, first[0] * 4 + first[1], second[0] * 4 + second[1], uo, m):
            ido[0:1, at:at + 128] = row

    def affinity(rows, n):
        lane0 = pl.multiple_of(2 * PAIR * n, 2 * PAIR)
        cosine = lax.dot_general(
            uc[rows, :], uo[pl.ds(lane0, 2 * PAIR), :], (((1,), (1,)), ((), ())),
            preferred_element_type=jnp.float32,
        )
        for at in range(rows.start, rows.stop, 16):
            part = slice(at, at + 16)
            total = racc[part, :]
            for t in range(6):
                lanes = pl.ds(pl.multiple_of(lane0 + 128 * t, 128), 128)
                piece = cosine[at - rows.start:at - rows.start + 16, 128 * t:128 * (t + 1)]
                weights = jnp.maximum(jnp.exp2(piece * SCALE) - THETA, 0.0)
                weights = jnp.where(idc[part, :] == ido[0:1, lanes], 0.0, weights)
                tile[part, lanes] = weights.astype(jnp.bfloat16)
                total = total + weights
            racc[part, :] = total

    first, second = slice(0, PAIR), slice(PAIR, 5 * PAIR)
    near, far = slice(0, 5 * PAIR), slice(5 * PAIR, 8 * PAIR)

    def take_plane(n):
        for s in XORDER[4 * n:4 * n + 4]:
            if s not in seen:
                plane[s].wait_recv()
        take_xy(2 * n)
        take_xy(2 * n + 1)

    seen = {(0, 0), (3, 0), (1, 0)}
    hop[7].wait_recv()
    relay(7)
    hop[1].wait_recv()
    relay(1)
    xbuf[0] = own[...]
    take_plane(0)
    take_z(0)
    affinity(first, 0)
    hop[6].wait_recv()
    zhop(6, 1)
    hop[2].wait_recv()
    zhop(2, -1)
    turn = jnp.where(lead, 6, 2)
    hop[4] = push(zblock(turn), zblock(4), 0, 4, zdev(jnp.where(lead, 2, NZ - 2), 0))
    relay(6)
    relay(2)
    plane[0, 1].wait_recv()
    phop(0, 1, 0, -1)
    plane[2, 0].wait_recv()
    for step in (1, -1, 2):
        phop(2, 0, 0, step)
    bases, handed = {}, {}

    def basis_to(dz):
        d = (NZ - dz) % NZ
        bases[d] = push(bown, bbuf.at[2 * d + k], 7, d, zdev(dz, 0))

    def basis_relay(d):
        if d:
            bases[d].wait_recv()
        handed[d] = push(bbuf.at[2 * d + k], bbuf.at[2 * d + k], 7, 8 + d, zdev(0, 1))

    for dz in (6, 2, 7, 1):
        basis_to(dz)
    seen |= {(0, 1), (2, 0)}

    for m in range(1, 5):
        take_z(m)
    affinity(second, 0)
    take_plane(1)
    affinity(near, 1)
    take_plane(2)
    affinity(near, 2)
    for d in (5, 3, 4):
        hop[d].wait_recv()
        relay(d)
    for dz in (4, 3, 5):
        basis_to(dz)
    for d in (0, 7, 1, 6, 2):
        basis_relay(d)
    take_plane(3)
    affinity(near, 3)
    for m in (5, 6, 7):
        take_z(m)

    def row_sums(ms):
        sums = {}
        for m in ms:
            for t in range(3):
                block = racc[PAIR * m + 128 * t:PAIR * m + 128 * (t + 1), :].T
                sums[3 * ((ZORDER[m] + 2) % NZ) + t] = jnp.sum(block, axis=0, keepdims=True)
        return sums

    for row, value in row_sums(range(5)).items():
        dnear[row:row + 1, :] = value
    dnear[15:16, :] = jnp.zeros((1, 128), jnp.float32)
    near_copies = {p: push(dnear, nbuf.at[zslot(*p)], 3, zslot(*p), zdev(*p)) for p in zpeers}

    def body(n, carry):
        affinity(far, 2 * n)
        affinity(far, 2 * n + 1)
        return carry

    lax.fori_loop(0, 2, body, 0)

    sums = row_sums(range(5, 8))
    rest = jnp.concatenate([sums[row] for row in range(15, 24)] + [jnp.zeros((7, 128), jnp.float32)], axis=0)
    dfar[...] = rest.astype(jnp.bfloat16)
    far_copies = {p: push(dfar, fbuf.at[zslot(*p)], 8, zslot(*p), zdev(*p)) for p in zpeers}
    for d in (5, 3, 4):
        basis_relay(d)
    degree = jnp.concatenate([dnear[0:15], rest[0:9]], axis=0)
    for dz in (0, 1, 7, 2, 6, 3, 5, 4):
        part = None
        for dk in ((1,) if dz == 0 else (0, 1)):
            near_copies[dz, dk].wait_recv()
            far_copies[dz, dk].wait_recv()
            slot = zslot(dz, dk)
            got = jnp.concatenate([nbuf[slot, 0:15], fbuf[slot].astype(jnp.float32)[0:9]], axis=0)
            part = got if part is None else part + got
        turn = 3 * dz
        if turn:
            part = jnp.concatenate([part[turn:24], part[0:turn]], axis=0)
        degree = degree + part
    dinv[...] = lax.rsqrt(1.0 + degree * (1.0 / THETA))

    for d in handed:
        handed[d].wait_recv()
    for m, d in enumerate(ZORDER):
        place = 3 * ((d + 2) % NZ)
        a, b = bbuf[2 * d].astype(jnp.float32), bbuf[2 * d + 1].astype(jnp.float32)
        pieces = (a[0:K], b[0:K], pair_tail(a[K:2 * K], b[K:2 * K]))
        for t, piece in enumerate(pieces):
            row = dinv[place + t:place + t + 1, :]
            scaled[:, PAIR * m + 128 * t:PAIR * m + 128 * (t + 1)] = (piece * row).astype(jnp.bfloat16)

    low = lax.broadcasted_iota(jnp.int32, (16, 128), 1) < 64
    copies = []
    for m in range(7, -1, -1):
        image = jnp.dot(scaled[...], tile[:, PAIR * m:PAIR * (m + 1)], preferred_element_type=jnp.float32)
        tails = image[:, 256:384]
        turned = pltpu.roll(tails, 64, 1)
        tail_a = jnp.where(low, tails[0:16], turned[16:32])
        tail_b = jnp.where(low, turned[0:16], tails[16:32])
        for (da, db), main, packed in ((XORDER[2 * m], image[:, 0:128], tail_a), (XORDER[2 * m + 1], image[:, 128:256], tail_b)):
            s = da * 4 + db
            isend[s, 0:32] = main.astype(isend.dtype)
            isend[s, 32:48] = packed.astype(isend.dtype)
            if s:
                t = xyslot(da, db)
                copies.append((t, push(isend.at[s], irecv.at[t], 4, t, xydev(da, db))))
            else:
                held = jnp.concatenate([main, packed], axis=0)
    for t, copy in copies:
        copy.wait_recv()
        held = held + irecv[t].astype(jnp.float32)
    low32 = lax.broadcasted_iota(jnp.int32, (K, 128), 1) < 64
    rest = held[32:48]
    rest = jnp.concatenate([rest, pltpu.roll(rest, 64, 1)], axis=0)
    dmain = dinv[pl.ds(6 + k, 1), :]
    dtail = dinv[8:9, :]
    dtail = jnp.where(k == 0, dtail, pltpu.roll(dtail, 64, 1))
    img0 = held[0:32] * (dmain * (1.0 / THETA))
    img1 = jnp.where(low32, rest * (dtail * (1.0 / THETA)), 0.0)

    nt = (((1,), (1,)), ((), ()))
    gram = lax.dot_general(img0, img0, nt, precision=HI, preferred_element_type=jnp.float32)
    gram = gram + lax.dot_general(img1, img1, nt, precision=HI, preferred_element_type=jnp.float32)
    gram = jnp.concatenate([gram[8 * g:8 * g + 8] for g in range(4)], axis=1)
    gsend[...] = gram
    copies = []
    for p in xypeers:
        s = xyslot(*p)
        copies.append((s, push(gsend, grecv.at[s], 5, s, xydev(*p))))
    for s, copy in copies:
        copy.wait_recv()
        gram = gram + grecv[s]
    hsend[...] = gram
    copies = []
    for p in zpeers:
        s = zslot(*p)
        copies.append((s, push(hsend, hrecv.at[s], 6, s, zdev(*p))))
    for s, copy in copies:
        copy.wait_recv()
    for s, copy in copies:
        gram = gram + hrecv[s]
    gram = jnp.concatenate([gram] + [pltpu.roll(gram, 128 - 32 * g, 1) for g in range(1, 4)], axis=0)

    lane = lax.broadcasted_iota(jnp.int32, (K, 128), 1)
    sub = lax.broadcasted_iota(jnp.int32, (K, 128), 0)
    side = jnp.where(lane < 64, img1, pltpu.roll(jnp.where(lane < 32, gram, 0.0), 64, 1))
    for j in range(0, K, 2):
        col_a = jnp.broadcast_to(side[:, 64 + j:65 + j], (K, 128))
        col_b = jnp.broadcast_to(side[:, 65 + j:66 + j], (K, 128))
        aa, ab, bb = col_a[j:j + 1], col_b[j:j + 1], col_b[j + 1:j + 2]
        ra = 1.0 / aa
        ratio = ab * ra
        rest = 1.0 / (bb - ab * ratio)
        fac_b = jnp.where(sub > j + 1, (col_b - col_a * ratio) * rest, 0.0)
        fac_a = jnp.where(sub > j, col_a * ra - fac_b * ratio, 0.0)
        img0 = img0 - (fac_a * img0[j:j + 1] + fac_b * img0[j + 1:j + 2])
        side = side - (fac_a * side[j:j + 1] + fac_b * side[j + 1:j + 2])
    diag = jnp.sum(jnp.where(lane == sub + 64, side, 0.0), axis=1, keepdims=True)
    final = lax.rsqrt(diag) * math.sqrt(NPTS)
    out[:, 0:128] = img0 * final
    out[:, 128:192] = (side * final)[:, 0:64]
    for copy in sends:
        copy.wait_send()


def on_device(embeddings, recordings, start_basis):
    f32, bf16 = jnp.float32, jnp.bfloat16
    return pl.pallas_call(
        kernel,
        out_shape=jax.ShapeDtypeStruct((K, SEG), f32),
        in_specs=[pl.BlockSpec(memory_space=pl.ANY)] * 3,
        out_specs=pl.BlockSpec(memory_space=pltpu.VMEM),
        scratch_shapes=[
            pltpu.VMEM((SEG, E), bf16),
            pltpu.VMEM((1, SEG), jnp.int32),
            pltpu.VMEM((K, SEG), bf16),
            pltpu.VMEM((16, XROWS, 128), bf16),
            pltpu.VMEM((16, XROWS, 128), bf16),
            pltpu.VMEM((16, 2 * K, 128), bf16),
            pltpu.VMEM((SIDE, 128), bf16),
            pltpu.VMEM((SIDE, 128), bf16),
            pltpu.VMEM((SIDE, 128), f32),
            pltpu.VMEM((8, SIDE), f32),
            pltpu.VMEM((SIDE, SIDE), bf16),
            pltpu.VMEM((SIDE, 128), f32),
            pltpu.VMEM((16, 128), f32),
            pltpu.VMEM((16, 128), bf16),
            pltpu.VMEM((16, 16, 128), f32),
            pltpu.VMEM((16, 16, 128), bf16),
            pltpu.VMEM((24, 128), f32),
            pltpu.VMEM((K, SIDE), bf16),
            pltpu.VMEM((16, 48, 128), bf16),
            pltpu.VMEM((16, 48, 128), bf16),
            pltpu.VMEM((8, 128), f32),
            pltpu.VMEM((16, 8, 128), f32),
            pltpu.VMEM((8, 128), f32),
            pltpu.VMEM((16, 8, 128), f32),
            pltpu.SemaphoreType.DMA((9, 16)),
            pltpu.SemaphoreType.DMA((9, 16)),
            pltpu.SemaphoreType.DMA((3,)),
        ],
        compiler_params=pltpu.CompilerParams(
            collective_id=0, has_side_effects=True, vmem_limit_bytes=63 * 2**20
        ),
    )(embeddings, recordings.reshape(1, SEG), start_basis)


def solution(mesh):
    in_specs = (P(("row", "col"), None), P(("row", "col")), P(None, ("row", "col")))
    out_specs = P(None, ("row", "col"))
    return jax.shard_map(
        on_device, mesh=mesh, in_specs=in_specs, out_specs=out_specs, check_vma=False
    )
```
